256 devices in a mesh: dp: 64 (over y, z, x_lo), mp: 4 (over x_hi, core).
Axes of the slice: x: 4 (x_hi: 2, x_lo: 2; x = x_hi * 2 + x_lo), y: 4, z: 8, core: 2. Of those that a mesh axis runs over, the one named last changes fastest.
Arguments:
- img_feat: bfloat16 [8192, 1536], P('dp', 'mp'), may hold values from -8 to 8
- txt_feat: bfloat16 [8192, 1152], P('dp', 'mp'), may hold values from -8 to 8
- img_proj: bfloat16 [1536, 1024], P('mp'), may hold values from -0.5 to 0.5
- txt_proj: bfloat16 [1152, 1024], P('mp'), may hold values from -0.5 to 0.5
- logit_scale: float32 [1], replicated, may hold values from 8 to 16
- logit_bias: float32 [1], replicated, may hold values from -8 to -3
Outputs:
- img_feat_grad: float32 [8192, 1536], P('dp', 'mp')
- txt_feat_grad: float32 [8192, 1152], P('dp', 'mp')
- img_proj_grad: float32 [1536, 1024], P('mp')
- txt_proj_grad: float32 [1152, 1024], P('mp')
The draws below stay inside these ranges and needn't reach their ends.
All inputs are finite; a program needn't handle non-finite values.
Results may differ from the reference program's by a relative error of at most 0.0025.
Values may be sent and summed in bfloat16 or wider, within the bound.
A program may use at most 64 MiB of HBM per device.

```python
import math
import jax
import jax.numpy as jnp
from jax import lax

E = 1024
DV = 1536
DT = 1152
BATCH = 8192


def shared_parts(key, lowest, highest):
    subkeys = jax.random.split(key, 4)
    centres = jax.random.normal(subkeys[0], (32, E), jnp.float32)
    labels = jax.random.randint(subkeys[1], (BATCH,), 0, 32)
    weights = jax.random.uniform(subkeys[2], (BATCH, 1), jnp.float32, lowest, highest)
    spread = jax.random.normal(subkeys[3], (BATCH, E), jnp.float32)
    picked = jnp.take(centres, labels, axis=0)
    return jnp.sqrt(1.0 - weights * weights) * spread + weights * picked


def shared_map(key):
    return jax.random.normal(jax.random.fold_in(key, 101), (E, E), jnp.float32)


def combine_parts(latent, jitter):
    leading = 0.8 * latent + 0.6 * jitter[:, :E]
    matrix = jnp.concatenate([leading, jitter[:, E:]], axis=1)
    return jnp.clip(matrix, -8.0, 8.0).astype(jnp.bfloat16)


def head_matrix(shared, private, bottom):
    upper_rows = shared + 0.3 * private
    matrix = jnp.concatenate([upper_rows, 0.5 * bottom], axis=0) * E ** (-0.5)
    return jnp.clip(matrix, -0.5, 0.5).astype(jnp.bfloat16)


def draw_img_feat(key, part):
    latent = shared_parts(key, 0.0, 0.9)
    key = jax.random.fold_in(key, 3)
    subkeys = jax.random.split(key, 1)
    jitter = jax.random.normal(subkeys[0], (BATCH, DV), jnp.float32)
    return combine_parts(latent, jitter)


def draw_txt_feat(key, part):
    latent = shared_parts(key, 0.0, 0.9)
    key = jax.random.fold_in(key, 5)
    subkeys = jax.random.split(key, 1)
    jitter = jax.random.normal(subkeys[0], (BATCH, DT), jnp.float32)
    return combine_parts(latent, jitter)


def draw_img_proj(key, part):
    shared = shared_map(key)
    key = jax.random.fold_in(key, 7)
    subkeys = jax.random.split(key, 2)
    private = jax.random.normal(subkeys[0], (E, E), jnp.float32)
    bottom = jax.random.normal(subkeys[1], (DV - E, E), jnp.float32)
    return head_matrix(shared, private, bottom)


def draw_txt_proj(key, part):
    shared = shared_map(key)
    key = jax.random.fold_in(key, 9)
    subkeys = jax.random.split(key, 2)
    private = jax.random.normal(subkeys[0], (E, E), jnp.float32)
    bottom = jax.random.normal(subkeys[1], (DT - E, E), jnp.float32)
    return head_matrix(shared, private, bottom)


def setup_inputs(seed: int = 0) -> dict:
    streams_of = jax.random.split(jax.random.key(seed), 7)
    img_feat = draw_img_feat(jax.random.fold_in(streams_of[6], 71), 0)
    txt_feat = draw_txt_feat(jax.random.fold_in(streams_of[6], 71), 0)
    img_proj = draw_img_proj(jax.random.fold_in(streams_of[6], 71), 0)
    txt_proj = draw_txt_proj(jax.random.fold_in(streams_of[6], 71), 0)
    logit_scale = jnp.clip(jax.random.uniform(streams_of[4], (1,), jnp.float32, 8.0, 16.0), 8.0, 16.0)
    logit_bias = jnp.clip(jax.random.uniform(streams_of[5], (1,), jnp.float32, -8.0, -3.0), -8.0, -3.0)
    return {"img_feat": img_feat, "txt_feat": txt_feat, "img_proj": img_proj, "txt_proj": txt_proj, "logit_scale": logit_scale, "logit_bias": logit_bias}


def normalize(full):
    norm = jnp.sqrt(lax.optimization_barrier(jnp.sum(full * full, axis=1, keepdims=True)) + 1e-06)
    return (full / norm, norm)

def back_norm(unit, norm, grad):
    inner = lax.optimization_barrier(jnp.sum(unit * grad, axis=1, keepdims=True))
    return ((grad - unit * inner) / norm).astype(jnp.bfloat16)

def reference(img_feat, txt_feat, img_proj, txt_proj, logit_scale, logit_bias):
    scale = logit_scale[0]
    offset = logit_bias[0]
    img_unit, img_norm = normalize(jnp.dot(img_feat, img_proj, preferred_element_type=jnp.float32))
    txt_unit, txt_norm = normalize(jnp.dot(txt_feat, txt_proj, preferred_element_type=jnp.float32))
    img_emb = img_unit.astype(jnp.bfloat16)
    txt_emb = txt_unit.astype(jnp.bfloat16)
    total = img_emb.shape[0]
    width = img_emb.shape[1]
    block_rows = math.gcd(512, total)
    blocks = total // block_rows
    text_ids = jnp.arange(total, dtype=jnp.int32)

    def one_block(acc, item):
        index, rows = item
        ids = index * block_rows + jnp.arange(block_rows, dtype=jnp.int32)
        logits = scale * jnp.dot(rows, txt_emb.T, preferred_element_type=jnp.float32) + offset
        sign = jnp.where(ids[:, None] == text_ids[None, :], jnp.float32(1.0), jnp.float32(-1.0))
        grad = (-sign * jax.nn.sigmoid(-sign * logits)).astype(jnp.bfloat16)
        img_term = scale * jnp.dot(grad, txt_emb, preferred_element_type=jnp.float32)
        acc = acc + scale * jnp.dot(grad.T, rows, preferred_element_type=jnp.float32)
        return (acc, img_term)
    zeros = jnp.zeros((total, width), jnp.float32)
    txt_grad, img_terms = lax.scan(one_block, zeros, (jnp.arange(blocks, dtype=jnp.int32), img_emb.reshape(blocks, block_rows, width)))
    img_grad = img_terms.reshape(total, width)
    img_du = back_norm(img_unit, img_norm, img_grad)
    txt_du = back_norm(txt_unit, txt_norm, txt_grad)
    root = jnp.sqrt(jnp.float32(total))
    img_feat_grad = jnp.dot(img_du, img_proj.T, preferred_element_type=jnp.float32)
    txt_feat_grad = jnp.dot(txt_du, txt_proj.T, preferred_element_type=jnp.float32)
    img_proj_grad = jnp.dot(img_feat.T, img_du, preferred_element_type=jnp.float32) / root
    txt_proj_grad = jnp.dot(txt_feat.T, txt_du, preferred_element_type=jnp.float32) / root
    return (img_feat_grad, txt_feat_grad, img_proj_grad, txt_proj_grad)
```

```python
import functools

import jax
import jax.numpy as jnp
from jax import lax
from jax.experimental import pallas as pl
from jax.experimental.pallas import tpu as pltpu
from jax.sharding import PartitionSpec as P

MESH = pl.DeviceIdType.MESH
F32 = jnp.float32
BF16 = jnp.bfloat16

NY, NZ, NXL, NXH, NC = 4, 8, 2, 2, 2
SIZE = {"y": NY, "z": NZ, "xl": NXL, "xh": NXH, "c": NC}
TEXT = ("xh", "xl", "y")
HEAD = ("z", "xl")
NTEXT = NXH * NXL * NY
NHEAD = NZ * NXL
MEMBERS = NXH * NC

NT = (((1,), (1,)), ((), ()))
TN = (((0,), (0,)), ((), ()))


def position():
    dp, mp = lax.axis_index("dp"), lax.axis_index("mp")
    return {
        "y": dp // (NZ * NXL),
        "z": (dp // NXL) % NZ,
        "xl": dp % NXL,
        "xh": mp // NC,
        "c": mp % NC,
    }


def shifted(me, axes, step, back=False):
    out = dict(me)
    for axis in reversed(axes):
        n = SIZE[axis]
        digit = lax.rem(step, n)
        step = step // n
        out[axis] = lax.rem(me[axis] + (n - digit if back else digit), n)
    return out


def address(at):
    return {
        "dp": (at["y"] * NZ + at["z"]) * NXL + at["xl"],
        "mp": at["xh"] * NC + at["c"],
    }


def send(src, dst, send_sem, recv_sem, to):
    return pltpu.make_async_remote_copy(
        src_ref=src,
        dst_ref=dst,
        send_sem=send_sem,
        recv_sem=recv_sem,
        device_id=address(to),
        device_id_type=MESH,
    )


def each(low, high, body):
    def step(k, _):
        body(k)
        return 0

    lax.fori_loop(low, high, step, 0)


def dot(a, b, dims=(((1,), (0,)), ((), ()))):
    return lax.dot_general(a, b, dims, preferred_element_type=F32)


def kernel(
    scale_ref, offset_ref, img_feat, txt_feat, img_proj, txt_proj,
    img_feat_out, txt_feat_out, img_proj_out, txt_proj_out,
    part, level1, relay, level2, unit, norm,
    img_emb, txt_emb, pair, sib_send, sib_recv,
    img_send, img_recv, txt_send, txt_recv, own,
    du, du_cols, img_all, txt_all, head_send, head_recv, heads,
    part_ss, part_rs, relay_ss, relay_rs, img_ss, img_rs, fwd_ss, fwd_rs, txt_ss, txt_rs,
    sib_ss, sib_rs, imgb_ss, imgb_rs, txtb_ss, txtb_rs, du_ss, du_rs, duf_ss, duf_rs,
    col_ss, col_rs, feat_ss, feat_rs, head_ss, head_rs, out_ss, out_rs, fin_ss, fin_rs,
):
    me = position()
    rows = unit.shape[1]
    width = unit.shape[2]
    cols = width // NY
    member = me["xh"] * NC + me["c"]
    scale = scale_ref[0]
    offset = offset_ref[0]
    sib = shifted(me, ("c",), 1)
    opp = shifted(me, ("xh",), 1)

    barrier = pltpu.get_barrier_semaphore()

    def greet(to):
        pl.semaphore_signal(barrier, inc=1, device_id=address(to), device_id_type=MESH)

    greet(sib)
    each(1, NZ, lambda k: greet(shifted(me, ("z",), k)))
    each(1, NTEXT, lambda k: greet(shifted(me, TEXT, k)))

    def greet_head(k):
        at = shifted(me, ("z",), k)
        greet(shifted(at, ("xl",), 1))

    each(0, NZ, greet_head)

    def partial(a, feat, proj):
        whole = dot(feat[...], proj[...])
        for q in range(MEMBERS):
            part[a, q % NC, q // NC] = whole[q * rows : (q + 1) * rows]

    partial(0, img_feat, img_proj)
    pl.semaphore_wait(barrier, 1 + (NZ - 1) + (NTEXT - 1) + NZ)

    def part_copy(a):
        return send(part.at[a, 1 - me["c"]], level1.at[a], part_ss.at[a], part_rs.at[a], sib)

    def relay_copy(a):
        return send(relay.at[a], level2.at[a], relay_ss.at[a], relay_rs.at[a], opp)

    part_copy(0).start()
    partial(1, txt_feat, txt_proj)
    part_copy(1).start()
    for a in range(2):
        part_copy(a).wait_recv()
        relay[a] = part[a, me["c"], 1 - me["xh"]] + level1[a, 1 - me["xh"]]
        relay_copy(a).start()

    img_all[0] = img_feat[...]
    txt_all[0] = txt_feat[...]

    def feat_copy(a, k):
        ref = (img_all, txt_all)[a]
        src = (img_feat, txt_feat)[a]
        return send(src, ref.at[k], feat_ss.at[a, k], feat_rs.at[a, k], shifted(me, ("y",), k))

    for a in range(2):
        each(1, NY, lambda k: feat_copy(a, k).start())

    def at_slot(k):
        return pl.ds(pl.multiple_of(k * rows, rows), rows)

    def embed(a, ref):
        relay_copy(a).wait_recv()
        full = part[a, me["c"], me["xh"]] + level1[a, me["xh"]] + level2[a]
        length = jnp.sqrt(jnp.sum(full * full, axis=1, keepdims=True) + 1e-06)
        value = full / length
        unit[a] = value
        norm[a] = jnp.broadcast_to(length, norm.shape[1:])
        ref[0:rows] = value.astype(BF16)

    def img_copy(k):
        return send(
            img_emb.at[0:rows], img_emb.at[at_slot(k)], img_ss.at[k], img_rs.at[k],
            shifted(me, ("z",), k),
        )

    def fwd_copy(k):
        return send(
            img_emb.at[at_slot(k)], img_emb.at[at_slot(NZ + k)], fwd_ss.at[k], fwd_rs.at[k], sib
        )

    def txt_copy(k):
        return send(
            txt_emb.at[0:rows], txt_emb.at[at_slot(k)], txt_ss.at[k], txt_rs.at[k],
            shifted(me, TEXT, k),
        )

    embed(0, img_emb)
    each(1, NZ, lambda k: img_copy(k).start())
    fwd_copy(0).start()
    embed(1, txt_emb)
    each(1, NTEXT, lambda k: txt_copy(k).start())

    def forward(k):
        img_copy(k).wait_recv()
        fwd_copy(k).start()

    each(1, NZ, forward)
    each(1, NTEXT, lambda k: txt_copy(k).wait_recv())
    each(0, NZ, lambda k: fwd_copy(k).wait_recv())

    half = NZ * rows
    txt_block = txt_emb[...]
    z = scale * dot(img_emb[...], txt_block, NT) + offset
    pair[...] = jax.nn.sigmoid(z).astype(BF16)
    corner = z[0:rows, 0:128]
    same = lax.broadcasted_iota(jnp.int32, corner.shape, 0) == lax.broadcasted_iota(
        jnp.int32, corner.shape, 1
    )
    pair[0:rows, 0:128] = jnp.where(
        same, -jax.nn.sigmoid(-corner), jax.nn.sigmoid(corner)
    ).astype(BF16)

    sib_copy = send(sib_send, sib_recv, sib_ss, sib_rs, sib)
    sib_send[...] = dot(pair[half : 2 * half], txt_block)
    sib_copy.start()

    def txtb_copy(k):
        return send(
            txt_send.at[at_slot(k)], txt_recv.at[k], txtb_ss.at[k], txtb_rs.at[k],
            shifted(me, TEXT, k, back=True),
        )

    def imgb_copy(k):
        return send(
            img_send.at[at_slot(k)], img_recv.at[k], imgb_ss.at[k], imgb_rs.at[k],
            shifted(me, ("z",), k, back=True),
        )

    txt_part = dot(pair[...], img_emb[...], TN)
    own[1] = txt_part[0:rows]
    txt_send[...] = txt_part.astype(BF16)
    each(1, NTEXT, lambda k: txtb_copy(k).start())
    img_part = dot(pair[0:half], txt_block)
    sib_copy.wait_recv()
    img_sum = img_part + sib_recv[...]
    own[0] = img_sum[0:rows]
    img_send[...] = img_sum.astype(BF16)
    each(1, NZ, lambda k: imgb_copy(k).start())

    def collect(a, copy, ref, count):
        def add(k, _):
            copy(k).wait_recv()
            own[a] += ref[k].astype(F32)
            return 0

        lax.fori_loop(1, count, add, 0)
        grad = scale * own[a]
        value = unit[a]
        inner = jnp.sum(value * grad, axis=1, keepdims=True)
        out = ((grad - value * inner) / norm[a, :, 0:1]).astype(BF16)
        for j in range(NY):
            du[member, j, a] = out[:, j * cols : (j + 1) * cols]

    collect(0, imgb_copy, img_recv, NZ)
    collect(1, txtb_copy, txt_recv, NTEXT)

    def block(q):
        return du.at[q]

    opp_copy = send(block(member), block(member), du_ss.at[0], du_rs.at[0], opp)
    near_copy = send(block(member), block(member), du_ss.at[1], du_rs.at[1], sib)
    far = opp["xh"] * NC + opp["c"]
    far_copy = send(block(far), block(far), duf_ss, duf_rs, sib)
    opp_copy.start()
    near_copy.start()
    opp_copy.wait_recv()
    far_copy.start()
    near_copy.wait_recv()
    far_copy.wait_recv()

    def col_copy(k):
        to = shifted(me, ("y",), k)
        return send(du.at[:, to["y"]], du_cols.at[k], col_ss.at[k], col_rs.at[k], to)

    each(1, NY, lambda k: col_copy(k).start())
    du_cols[0] = du[:, me["y"]]

    group = MEMBERS * rows
    for a, proj, out in ((0, img_proj, img_feat_out), (1, txt_proj, txt_feat_out)):
        total = None
        for j in range(NY):
            term = dot(du[:, j, a].reshape(group, cols), proj[:, j * cols : (j + 1) * cols], NT)
            total = term if total is None else total + term
        out[...] = total

    for a in range(2):
        each(1, NY, lambda k: feat_copy(a, k).wait_recv())
    each(1, NY, lambda k: col_copy(k).wait_recv())

    lanes = cols // NXL
    img_rows = img_proj_out.shape[0] // NZ
    piece = head_send.shape[2]
    txt_rows = piece - img_rows
    txt_holders = txt_proj_out.shape[0] // txt_rows

    def weight(a, ref):
        total = None
        for k in range(NY):
            term = dot(ref[k], du_cols[k, :, a].reshape(group, cols), TN)
            total = term if total is None else total + term
        return total

    root = jnp.sqrt(F32(group * NY * NZ * NXL))
    img_weight = weight(0, img_all).astype(BF16)
    txt_weight = weight(1, txt_all).astype(BF16)
    for s in range(NXL):
        for h in range(NZ):
            head_send[s, h, 0:img_rows] = img_weight[
                h * img_rows : (h + 1) * img_rows, s * lanes : (s + 1) * lanes
            ]
            if h < txt_holders:
                head_send[s, h, img_rows:piece] = txt_weight[
                    h * txt_rows : (h + 1) * txt_rows, s * lanes : (s + 1) * lanes
                ]
            else:
                head_send[s, h, img_rows:piece] = jnp.zeros((txt_rows, lanes), BF16)

    def head_copy(k):
        to = shifted(me, HEAD, k)
        return send(
            head_send.at[to["xl"], to["z"]], head_recv.at[k], head_ss.at[k], head_rs.at[k], to
        )

    each(1, NHEAD, lambda k: head_copy(k).start())

    def head_add(k, total):
        head_copy(k).wait_recv()
        return total + head_recv[k].astype(F32)

    total = lax.fori_loop(1, NHEAD, head_add, head_send[me["xl"], me["z"]].astype(F32))
    heads[me["y"], me["xl"], me["z"]] = (total / root).astype(BF16)

    def out_copy(k):
        at = heads.at[me["y"], me["xl"], me["z"]]
        return send(at, at, out_ss.at[k], out_rs.at[k], shifted(me, HEAD, k))

    def out_arrival(k):
        frm = shifted(me, HEAD, k, back=True)
        at = heads.at[me["y"], frm["xl"], frm["z"]]
        return send(at, at, out_ss.at[k], out_rs.at[k], shifted(me, HEAD, k))

    each(1, NHEAD, lambda k: out_copy(k).start())
    each(1, NHEAD, lambda k: out_arrival(k).wait_recv())

    def fin_copy(k):
        at = heads.at[me["y"]]
        return send(at, at, fin_ss.at[k], fin_rs.at[k], shifted(me, ("y",), k))

    def fin_arrival(k):
        at = heads.at[shifted(me, ("y",), k, back=True)["y"]]
        return send(at, at, fin_ss.at[k], fin_rs.at[k], shifted(me, ("y",), k))

    each(1, NY, lambda k: fin_copy(k).start())
    each(1, NY, lambda k: fin_arrival(k).wait_recv())
    for j in range(NY):
        for s in range(NXL):
            lane = slice((j * NXL + s) * lanes, (j * NXL + s + 1) * lanes)
            for h in range(NZ):
                img_proj_out[h * img_rows : (h + 1) * img_rows, lane] = heads[j, s, h, 0:img_rows]
                if h < txt_holders:
                    txt_proj_out[h * txt_rows : (h + 1) * txt_rows, lane] = heads[
                        j, s, h, img_rows:piece
                    ]

    for a in range(2):
        part_copy(a).wait_send()
        relay_copy(a).wait_send()
        each(1, NY, lambda k: feat_copy(a, k).wait_send())
    each(1, NZ, lambda k: img_copy(k).wait_send())
    each(0, NZ, lambda k: fwd_copy(k).wait_send())
    each(1, NTEXT, lambda k: txt_copy(k).wait_send())
    sib_copy.wait_send()
    each(1, NZ, lambda k: imgb_copy(k).wait_send())
    each(1, NTEXT, lambda k: txtb_copy(k).wait_send())
    opp_copy.wait_send()
    near_copy.wait_send()
    far_copy.wait_send()
    each(1, NY, lambda k: col_copy(k).wait_send())
    each(1, NHEAD, lambda k: head_copy(k).wait_send())
    each(1, NHEAD, lambda k: out_copy(k).wait_send())
    each(1, NY, lambda k: fin_copy(k).wait_send())


def local(img_feat, txt_feat, img_proj, txt_proj, logit_scale, logit_bias):
    group, img_width = img_feat.shape
    txt_width = txt_feat.shape[1]
    width = img_proj.shape[1]
    rows = group // MEMBERS
    cols = width // NY
    lanes = cols // NXL
    img_rows = img_width // NZ
    txt_rows = -(-txt_width // NZ // 16) * 16
    piece = img_rows + txt_rows
    dma = pltpu.SemaphoreType.DMA
    vmem = pltpu.VMEM

    def pair(*shape):
        return [dma(shape), dma(shape)]

    scratch = [
        vmem((2, NC, NXH, rows, width), F32),
        vmem((2, NXH, rows, width), F32),
        vmem((2, rows, width), F32),
        vmem((2, rows, width), F32),
        vmem((2, rows, width), F32),
        vmem((2, rows, 128), F32),
        vmem((NC * NZ * rows, width), BF16),
        vmem((NTEXT * rows, width), BF16),
        vmem((NC * NZ * rows, NTEXT * rows), BF16),
        vmem((NZ * rows, width), F32),
        vmem((NZ * rows, width), F32),
        vmem((NZ * rows, width), BF16),
        vmem((NZ, rows, width), BF16),
        vmem((NTEXT * rows, width), BF16),
        vmem((NTEXT, rows, width), BF16),
        vmem((2, rows, width), F32),
        vmem((MEMBERS, NY, 2, rows, cols), BF16),
        vmem((NY, MEMBERS, 2, rows, cols), BF16),
        vmem((NY, group, img_width), BF16),
        vmem((NY, group, txt_width), BF16),
        vmem((NXL, NZ, piece, lanes), BF16),
        vmem((NHEAD, piece, lanes), BF16),
        vmem((NY, NXL, NZ, piece, lanes), BF16),
        *pair(2), *pair(2), *pair(NZ), *pair(NZ), *pair(NTEXT),
        dma(()), dma(()), *pair(NZ), *pair(NTEXT), *pair(2), dma(()), dma(()),
        *pair(NY), *pair(2, NY), *pair(NHEAD), *pair(NHEAD), *pair(NY),
    ]
    in_vmem = pl.BlockSpec(memory_space=pltpu.VMEM)
    in_smem = pl.BlockSpec(memory_space=pltpu.SMEM)
    img_grad, txt_grad, img_sum, txt_sum = pl.pallas_call(
        kernel,
        out_shape=(
            jax.ShapeDtypeStruct((group, img_width), F32),
            jax.ShapeDtypeStruct((group, txt_width), F32),
            jax.ShapeDtypeStruct((img_width, width), BF16),
            jax.ShapeDtypeStruct((txt_width, width), BF16),
        ),
        in_specs=[in_smem, in_smem] + [in_vmem] * 4,
        out_specs=(in_vmem,) * 4,
        scratch_shapes=scratch,
        compiler_params=pltpu.CompilerParams(
            collective_id=0, has_side_effects=True, vmem_limit_bytes=48 * 2**20
        ),
        name="pair_loss",
    )(logit_scale, logit_bias, img_feat, txt_feat, img_proj, txt_proj)
    return img_grad, txt_grad, img_sum.astype(F32), txt_sum.astype(F32)


def solution(mesh):
    placed = (P("dp", "mp"), P("dp", "mp"), P("mp", None), P("mp", None), P(), P())
    return jax.shard_map(
        local,
        mesh=mesh,
        in_specs=placed,
        out_specs=(P("dp", "mp"), P("dp", "mp"), P("mp", None), P("mp", None)),
        check_vma=False,
    )
```
